32 devices in a mesh: copies: 2 (over y), sector: 4 (over z), inner: 2 (over x), pair: 2 (over core).
Axes of the slice: x: 2, y: 2, z: 4, core: 2. Of those that a mesh axis runs over, the one named last changes fastest.
Arguments:
- wave_blocks: bfloat16 [8, 512, 512], P(('copies', 'sector'), 'inner'), parts along dimension 0, may hold values from -6 to 6
- left_env: bfloat16 [8, 12, 512, 512], P(('copies', 'sector'), None, 'inner'), parts along dimension 0, may hold values from -0.078125 to 0.078125
- right_env: bfloat16 [8, 12, 512, 512], P(('copies', 'sector'), None, 'pair'), parts along dimension 0, may hold values from -0.25 to 0.25
- source_pairs: int32 [8, 12], P(('copies', 'sector')), parts along dimension 0, may hold values from 0 to 3
- block_sizes: int32 [8], P('copies'), parts along dimension 0, may hold values from 64 to 512, as said below
Outputs:
- sigma_first: bfloat16 [8, 512, 512], P(('copies', 'sector'), 'inner', 'pair'), parts along dimension 0
- sigma_second: bfloat16 [8, 512, 512], P(('copies', 'sector'), 'inner', 'pair'), parts along dimension 0
The draws below stay inside these ranges and needn't reach their ends.
There are 2 independent parts, one for each index of `copies`. The reference program is written for one: setup_inputs(seed, part) draws one part's arguments, and reference() takes and returns one part's arrays. A program takes and returns all parts, laid end to end along the dimension named above; each array names one. Nothing has to cross between parts.
Inputs may be any that keep to these rules, and one draw needn't show every extreme that they name: `block_sizes`: each entry is a multiple of 64.
All inputs are finite; a program needn't handle non-finite values.
Results may differ from the reference program's by a relative error of at most 0.007.
Values may be sent and summed in bfloat16 or wider, within the bound.
A program may use at most 64 MiB of HBM per device.

```python
import jax
import jax.numpy as jnp
from jax import lax

B = 512
KP = 12
NSEC = 4


def draw_block_sizes(key, part):
    key = jax.random.fold_in(key, 5)
    order_key, unit_key = jax.random.split(key)
    order = jax.random.permutation(order_key, NSEC)
    units = jax.random.randint(unit_key, (NSEC,), 1, 9, dtype=jnp.int32)
    units = jnp.where(order == 0, 1, jnp.where(order == 1, 8, units))
    return (units * (B // 8)).astype(jnp.int32)


def place_ends(entries, own_key, low, largest):
    index_at = [jax.random.randint(jax.random.fold_in(own_key, axis), (), 0, length) for axis, length in enumerate(entries.shape)]
    widest = entries.shape.index(max(entries.shape))
    next_to = index_at[:widest] + [(index_at[widest] + 1) % entries.shape[widest]] + index_at[widest + 1:]
    return entries.at[tuple(index_at)].set(low).at[tuple(next_to)].set(largest)


def steps_of(stream_key, shape, shards, least, top_value):
    def one(dim, shards_of):
        steps = jax.random.uniform(jax.random.fold_in(jax.random.fold_in(stream_key, 6), dim), (shards_of,), jnp.float32, least / len(shards), top_value / len(shards))
        return jnp.repeat(jnp.exp(steps), shape[dim] // shards_of).reshape((-1,) + (1,) * (len(shape) - dim - 1))

    gain = one(*shards[0])
    for cut in shards[1:]:
        gain = gain * one(*cut)
    return gain


def gaussian(rng, dims, deviation, most, cuts=(), held_as=jnp.bfloat16):
    values = deviation * jax.random.normal(rng, dims, jnp.float32)
    if cuts:
        values = values * steps_of(rng, dims, cuts, -0.22, 0.18)
    return jnp.clip(values, -most, most).astype(held_as)


def setup_inputs(seed: int = 0, part: int = 0) -> dict:
    streams_of = jax.random.split(jax.random.key(seed), 6)
    own_keys = jax.random.split(jax.random.fold_in(streams_of[5], part), 6)
    return {
        "wave_blocks": gaussian(own_keys[0], (NSEC, B, B), 1.0, 6.0, ((0, 4), (1, 2))),
        "left_env": gaussian(own_keys[1], (NSEC, KP, B, B), (B * KP) ** -0.5, 0.078125, ((0, 4), (2, 2))),
        "right_env": gaussian(own_keys[2], (NSEC, KP, B, B), B ** -0.5, 0.25, ((0, 4), (2, 2))),
        "source_pairs": place_ends(jax.random.randint(own_keys[3], (NSEC, KP), 0, NSEC), jax.random.fold_in(own_keys[3], 1), 0, NSEC - 1).astype(jnp.int32),
        "block_sizes": draw_block_sizes(jax.random.fold_in(jax.random.fold_in(streams_of[5], part), 71), part),
    }


def reference(wave_blocks, left_env, right_env, source_pairs, block_sizes):
    index = jnp.arange(B, dtype=jnp.int32)
    block_mask = ((index[None, :, None] < block_sizes[:, None, None]) & (index[None, None, :] < block_sizes[:, None, None])).astype(jnp.float32)
    masked = (wave_blocks.astype(jnp.float32) * block_mask).astype(jnp.bfloat16)

    def apply_field(field):

        def per_sector(sector):
            sources = jnp.take(field, source_pairs[sector], axis=0).astype(jnp.float32)
            halfway = jnp.einsum('kar,kbr->kab', sources, right_env[sector].astype(jnp.float32)).astype(jnp.bfloat16)
            product = jnp.einsum('kam,kmb->ab', left_env[sector].astype(jnp.float32), halfway.astype(jnp.float32))
            return (product * block_mask[sector]).astype(jnp.bfloat16)
        return lax.map(per_sector, jnp.arange(NSEC, dtype=jnp.int32))
    sigma_first = apply_field(masked)
    wave_wide = masked.astype(jnp.float32)
    sigma_wide = sigma_first.astype(jnp.float32)
    self_norm = jnp.sum(wave_wide * wave_wide)
    correlation_sum = jnp.sum(wave_wide * sigma_wide)
    rayleigh = correlation_sum / self_norm
    residual = sigma_wide - rayleigh * wave_wide
    residual_sq = jnp.sum(residual * residual)
    correction = (residual * lax.rsqrt(residual_sq / (NSEC * B * B) + 1e-06)).astype(jnp.bfloat16)
    sigma_second = apply_field(correction)
    return (sigma_first, sigma_second)
```

```python
import functools

import jax
import jax.numpy as jnp
from jax import lax
from jax.experimental import pallas as pl
from jax.experimental.pallas import tpu as pltpu
from jax.sharding import PartitionSpec as P

MESH = pl.DeviceIdType.MESH


def kernel(
    sectors, inners, wave_ref, left_hbm, right_hbm, src_ref, size_ref, first_ref, second_ref,
    field, sigma, left_ref, right_ref, total, load_sem, send_sem, recv_sem,
):
    _, rows, width = wave_ref.shape
    terms, cols = right_ref.shape[0], right_ref.shape[1]
    s = lax.axis_index("sector")
    i = lax.axis_index("inner")
    p = lax.axis_index("pair")
    other = 1 - p
    after = [lax.rem(i + step, inners) for step in range(1, inners)]
    before = [lax.rem(i + inners - step, inners) for step in range(1, inners)]

    loads = (
        pltpu.make_async_copy(left_hbm.at[0], left_ref, load_sem.at[0]),
        pltpu.make_async_copy(right_hbm.at[0], right_ref, load_sem.at[1]),
    )
    for load in loads:
        load.start()

    barrier = pltpu.get_barrier_semaphore()
    for step in range(1, sectors):
        there = lax.rem(s + step, sectors)
        pl.semaphore_signal(barrier, inc=1, device_id={"sector": there}, device_id_type=MESH)
    for there in after:
        pl.semaphore_signal(barrier, inc=1, device_id={"inner": there}, device_id_type=MESH)
    pl.semaphore_signal(barrier, inc=1, device_id={"pair": other}, device_id_type=MESH)

    def part(buffer, half, sector, inner):
        start = pl.multiple_of(inner * rows, rows)
        return buffer.at[half, sector, pl.ds(start, rows), :]

    size = size_ref[s]
    own_row = pl.multiple_of(i * rows, rows)
    row_ids = own_row + lax.broadcasted_iota(jnp.int32, (rows, cols), 0)
    col_ids = lax.broadcasted_iota(jnp.int32, (rows, cols), 1)
    row_live = row_ids < size
    for half in range(width // cols):
        live = row_live & (col_ids + half * cols < size)
        piece = wave_ref[0, :, half * cols:(half + 1) * cols].astype(jnp.float32)
        field[half, s, pl.ds(own_row, rows), :] = jnp.where(live, piece, 0.0).astype(jnp.bfloat16)

    pl.semaphore_wait(barrier, sectors + inners - 1)

    def gather(buffer, phase, share_own):
        started = []

        def send(cond, half, sector, inner, to):
            number = len(started)

            def make():
                ref = part(buffer, half, sector, inner)
                return pltpu.make_async_remote_copy(
                    src_ref=ref, dst_ref=ref, send_sem=send_sem.at[phase, number],
                    recv_sem=recv_sem.at[phase, half, sector, inner],
                    device_id=to, device_id_type=MESH,
                )

            started.append((cond, make))
            make().start()

        def arrive(half, sector, inner):
            ref = part(buffer, half, sector, inner)
            pltpu.make_async_remote_copy(
                src_ref=ref, dst_ref=ref, send_sem=send_sem.at[phase, 0],
                recv_sem=recv_sem.at[phase, half, sector, inner],
                device_id={"pair": other}, device_id_type=MESH,
            ).wait_recv()

        def guarded(cond, work):
            if cond is None:
                work()
            else:
                pl.when(cond)(work)

        def spread(cond, sector):
            for there in after:
                send(cond, p, sector, i, {"inner": there})

        def from_inner(cond, sector):
            def work():
                for there in before:
                    arrive(p, sector, there)
                    send(cond, p, sector, there, {"pair": other})
            guarded(cond, work)

        has_up, has_down = s + 1 < sectors, s >= 1
        up, down = s + 1, s - 1
        pl.when(has_up)(lambda: send(has_up, p, s, i, {"sector": up}))
        pl.when(has_down)(lambda: send(has_down, p, s, i, {"sector": down}))
        spread(None, s)
        if share_own:
            send(None, p, s, i, {"pair": other})

        def from_sector(cond, sector, further, onward):
            both = cond & onward

            def work():
                arrive(p, sector, i)
                pl.when(onward)(lambda: send(both, p, sector, i, {"sector": further}))
                spread(cond, sector)
                send(cond, p, sector, i, {"pair": other})
            guarded(cond, work)

        late = [(None, s)]
        for step in range(1, sectors):
            below, above = s - step >= 0, s + step < sectors
            from_sector(below, s - step, up, has_up)
            from_sector(above, s + step, down, has_down)
            for cond, sector in late:
                from_inner(cond, sector)
            late = [(below, s - step), (above, s + step)]
        for cond, sector in late:
            from_inner(cond, sector)

        for sector in range(sectors):
            for inner in range(inners):
                if share_own:
                    arrive(other, sector, inner)
                else:
                    pl.when((sector != s) | (inner != i))(
                        functools.partial(arrive, other, sector, inner)
                    )
        for cond, make in started:
            guarded(cond, lambda make=make: make().wait_send())

    def dot(a, b, dims):
        return lax.dot_general(a, b, (dims, ((), ())), preferred_element_type=jnp.float32)

    def apply():
        total[...] = jnp.zeros_like(total)

        def term(k, carry):
            source = src_ref[0, k]
            half = sum(
                dot(field[q, source], right_ref[k, :, q * cols:(q + 1) * cols], ((1,), (1,)))
                for q in range(width // cols)
            ).astype(jnp.bfloat16)
            total[...] += dot(left_ref[k], half, ((1,), (0,)))
            return carry

        lax.fori_loop(0, terms, term, 0, unroll=2)
        live = row_live & (col_ids + p * cols < size)
        return jnp.where(live, total[...], 0.0).astype(jnp.bfloat16)

    gather(field, 0, False)
    for load in loads:
        load.wait()
    first = apply()
    first_ref[0] = first
    sigma[p, s, pl.ds(own_row, rows), :] = first
    gather(sigma, 1, True)

    blocks = [(q, t) for q in range(width // cols) for t in range(sectors)]

    def fold(x):
        return jnp.sum(x.reshape(-1, 8, cols), axis=0)

    def sums(n, carry):
        q, t = n // sectors, lax.rem(n, sectors)
        w = field[q, t].astype(jnp.float32)
        g = sigma[q, t].astype(jnp.float32)
        return (carry[0] + fold(w * w), carry[1] + fold(w * g), carry[2] + fold(g * g))

    zero = jnp.zeros((8, cols), jnp.float32)
    self_norm, correlation, sigma_norm = (
        jnp.sum(x) for x in lax.fori_loop(0, len(blocks), sums, (zero, zero, zero))
    )
    self_norm, correlation, sigma_norm = (
        jnp.full((8, cols), x, jnp.float32) for x in (self_norm, correlation, sigma_norm)
    )
    rayleigh = correlation / self_norm
    residual_sq = sigma_norm - 2.0 * rayleigh * correlation + rayleigh * rayleigh * self_norm
    scale = lax.rsqrt(residual_sq / (sectors * width * width) + 1e-06)
    rayleigh, scale = rayleigh[:1], scale[:1]

    def correct(n, carry):
        q, t = n // sectors, lax.rem(n, sectors)
        w = field[q, t].astype(jnp.float32)
        g = sigma[q, t].astype(jnp.float32)
        field[q, t] = ((g - rayleigh * w) * scale).astype(jnp.bfloat16)
        return carry

    lax.fori_loop(0, len(blocks), correct, 0)
    second_ref[0] = apply()


def body(wave_blocks, left_env, right_env, source_pairs, block_sizes):
    _, rows, width = wave_blocks.shape
    terms, cols = right_env.shape[1], right_env.shape[2]
    sectors, inners = lax.axis_size("sector"), lax.axis_size("inner")
    copies = 2 * (sectors + 1) * (inners + 1) + 2 * sectors * inners
    out = jax.ShapeDtypeStruct((1, rows, cols), jnp.bfloat16)
    vmem = pl.BlockSpec(memory_space=pltpu.VMEM)
    smem = pl.BlockSpec(memory_space=pltpu.SMEM)
    hbm = pl.BlockSpec(memory_space=pl.ANY)
    return pl.pallas_call(
        functools.partial(kernel, sectors, inners),
        out_shape=(out, out),
        in_specs=[vmem, hbm, hbm, smem, smem],
        out_specs=(vmem, vmem),
        scratch_shapes=[
            pltpu.VMEM((width // cols, sectors, width, cols), jnp.bfloat16),
            pltpu.VMEM((width // cols, sectors, width, cols), jnp.bfloat16),
            pltpu.VMEM(left_env.shape[1:], jnp.bfloat16),
            pltpu.VMEM(right_env.shape[1:], jnp.bfloat16),
            pltpu.VMEM((rows, cols), jnp.float32),
            pltpu.SemaphoreType.DMA((2,)),
            pltpu.SemaphoreType.DMA((2, copies)),
            pltpu.SemaphoreType.DMA((2, width // cols, sectors, inners)),
        ],
        compiler_params=pltpu.CompilerParams(
            collective_id=0, has_side_effects=True, vmem_limit_bytes=56 * 1024 * 1024
        ),
    )(wave_blocks, left_env, right_env, source_pairs, block_sizes)


def solution(mesh):
    return jax.shard_map(
        body,
        mesh=mesh,
        in_specs=(
            P(("copies", "sector"), "inner", None),
            P(("copies", "sector"), None, "inner", None),
            P(("copies", "sector"), None, "pair", None),
            P(("copies", "sector"), None),
            P("copies"),
        ),
        out_specs=(
            P(("copies", "sector"), "inner", "pair"),
            P(("copies", "sector"), "inner", "pair"),
        ),
        check_vma=False,
    )
```

```python
import functools

import jax
import jax.numpy as jnp
from jax import lax
from jax.experimental import pallas as pl
from jax.experimental.pallas import tpu as pltpu
from jax.sharding import PartitionSpec as P

MESH = pl.DeviceIdType.MESH


def kernel(
    sectors, inners, chunks, wave_ref, left_hbm, right_hbm, src_ref, size_ref, first_ref, second_ref,
    field, sigma, left_ref, right_ref, total, load_sem, send_sem, recv_sem,
):
    _, rows, width = wave_ref.shape
    terms, cols = right_ref.shape[0], right_ref.shape[1]
    s = lax.axis_index("sector")
    i = lax.axis_index("inner")
    p = lax.axis_index("pair")
    other = 1 - p
    after = [lax.rem(i + step, inners) for step in range(1, inners)]
    before = [lax.rem(i + inners - step, inners) for step in range(1, inners)]

    loads = (
        pltpu.make_async_copy(left_hbm.at[0], left_ref, load_sem.at[0]),
        pltpu.make_async_copy(right_hbm.at[0], right_ref, load_sem.at[1]),
    )
    for load in loads:
        load.start()

    barrier = pltpu.get_barrier_semaphore()
    up, down = s + 1, s - 1
    has_up, has_down = up < sectors, down >= 0
    for near, there in ((has_up, up), (has_down, down)):
        @pl.when(near)
        def _(there=there):
            pl.semaphore_signal(barrier, inc=1, device_id={"sector": there}, device_id_type=MESH)
    for there in after:
        pl.semaphore_signal(barrier, inc=1, device_id={"inner": there}, device_id_type=MESH)
    pl.semaphore_signal(barrier, inc=1, device_id={"pair": other}, device_id_type=MESH)

    depth = rows // chunks

    def part(buffer, half, sector, inner, chunk):
        start = pl.multiple_of(inner * rows + chunk * depth, depth)
        return buffer.at[half, sector, pl.ds(start, depth), :]

    size = size_ref[s]
    own_row = pl.multiple_of(i * rows, rows)
    row_ids = own_row + lax.broadcasted_iota(jnp.int32, (rows, cols), 0)
    col_ids = lax.broadcasted_iota(jnp.int32, (rows, cols), 1)
    row_live = row_ids < size
    for half in range(width // cols):
        live = row_live & (col_ids + half * cols < size)
        piece = wave_ref[0, :, half * cols:(half + 1) * cols].astype(jnp.float32)
        field[half, s, pl.ds(own_row, rows), :] = jnp.where(live, piece, 0.0).astype(jnp.bfloat16)

    ends = lax.div(s + sectors - 1, sectors) + lax.div(2 * sectors - 2 - s, sectors)
    pl.semaphore_wait(barrier, inners + ends)

    def guarded(cond, work):
        if cond is None:
            work()
        else:
            pl.when(cond)(work)

    def gather(buffer, phase, share_own):
        started = []

        def send(cond, half, sector, inner, chunk, to):
            number = len(started)

            def make():
                ref = part(buffer, half, sector, inner, chunk)
                return pltpu.make_async_remote_copy(
                    src_ref=ref, dst_ref=ref, send_sem=send_sem.at[phase, number],
                    recv_sem=recv_sem.at[phase, chunk, half, sector, inner],
                    device_id=to, device_id_type=MESH,
                )

            started.append((cond, make))
            make().start()

        def arrive(half, sector, inner, chunk):
            ref = part(buffer, half, sector, inner, chunk)
            pltpu.make_async_remote_copy(
                src_ref=ref, dst_ref=ref, send_sem=send_sem.at[phase, 0],
                recv_sem=recv_sem.at[phase, chunk, half, sector, inner],
                device_id={"pair": other}, device_id_type=MESH,
            ).wait_recv()

        def spread(cond, sector, chunk):
            for there in after:
                send(cond, p, sector, i, chunk, {"inner": there})

        def from_inner(cond, sector, chunk):
            def work():
                for there in before:
                    arrive(p, sector, there, chunk)
                    send(cond, p, sector, there, chunk, {"pair": other})
            guarded(cond, work)

        def from_sector(cond, sector, further, onward, chunk):
            both = cond & onward

            def work():
                arrive(p, sector, i, chunk)
                pl.when(onward)(lambda: send(both, p, sector, i, chunk, {"sector": further}))
                spread(cond, sector, chunk)
                send(cond, p, sector, i, chunk, {"pair": other})
            guarded(cond, work)

        for chunk in range(chunks):
            pl.when(has_up)(lambda: send(has_up, p, s, i, chunk, {"sector": up}))
            pl.when(has_down)(lambda: send(has_down, p, s, i, chunk, {"sector": down}))
            spread(None, s, chunk)
            if share_own:
                send(None, p, s, i, chunk, {"pair": other})

        late = [(None, s)]
        for step in range(1, sectors):
            below, above = s - step >= 0, s + step < sectors
            arriving = [(below, s - step), (above, s + step)]
            for chunk in range(chunks):
                from_sector(*arriving[0], up, has_up, chunk)
                from_sector(*arriving[1], down, has_down, chunk)
                for cond, sector in late:
                    from_inner(cond, sector, chunk)
            late = arriving
        for chunk in range(chunks):
            for cond, sector in late:
                from_inner(cond, sector, chunk)

        for sector in range(sectors):
            for inner in range(inners):
                for chunk in range(chunks):
                    wait = functools.partial(arrive, other, sector, inner, chunk)
                    guarded(None if share_own else (sector != s) | (inner != i), wait)
        for cond, make in started:
            guarded(cond, lambda make=make: make().wait_send())

    def dot(a, b, dims):
        return lax.dot_general(a, b, (dims, ((), ())), preferred_element_type=jnp.float32)

    def apply():
        total[...] = jnp.zeros_like(total)

        def term(k, carry):
            source = src_ref[0, k]
            half = sum(
                dot(field[q, source], right_ref[k, :, q * cols:(q + 1) * cols], ((1,), (1,)))
                for q in range(width // cols)
            ).astype(jnp.bfloat16)
            total[...] += dot(left_ref[k], half, ((1,), (0,)))
            return carry

        lax.fori_loop(0, terms, term, 0, unroll=terms)
        live = row_live & (col_ids + p * cols < size)
        return jnp.where(live, total[...], 0.0).astype(jnp.bfloat16)

    gather(field, 0, False)
    for load in loads:
        load.wait()
    first = apply()
    first_ref[0] = first
    sigma[p, s, pl.ds(own_row, rows), :] = first
    gather(sigma, 1, True)

    blocks = [(q, t) for q in range(width // cols) for t in range(sectors)]

    def fold(x):
        return jnp.sum(x.reshape(-1, 8, cols), axis=0)

    def sums(n, carry):
        q, t = n // sectors, lax.rem(n, sectors)
        w = field[q, t].astype(jnp.float32)
        g = sigma[q, t].astype(jnp.float32)
        return (carry[0] + fold(w * w), carry[1] + fold(w * g), carry[2] + fold(g * g))

    zero = jnp.zeros((8, cols), jnp.float32)
    self_norm, correlation, sigma_norm = (
        jnp.sum(x) for x in lax.fori_loop(0, len(blocks), sums, (zero, zero, zero))
    )
    self_norm, correlation, sigma_norm = (
        jnp.full((8, cols), x, jnp.float32) for x in (self_norm, correlation, sigma_norm)
    )
    rayleigh = correlation / self_norm
    residual_sq = sigma_norm - 2.0 * rayleigh * correlation + rayleigh * rayleigh * self_norm
    scale = lax.rsqrt(residual_sq / (sectors * width * width) + 1e-06)
    rayleigh, scale = rayleigh[:1], scale[:1]

    def correct(n, carry):
        q, t = n // sectors, lax.rem(n, sectors)
        w = field[q, t].astype(jnp.float32)
        g = sigma[q, t].astype(jnp.float32)
        field[q, t] = ((g - rayleigh * w) * scale).astype(jnp.bfloat16)
        return carry

    lax.fori_loop(0, len(blocks), correct, 0)
    second_ref[0] = apply()


def body(wave_blocks, left_env, right_env, source_pairs, block_sizes):
    _, rows, width = wave_blocks.shape
    terms, cols = right_env.shape[1], right_env.shape[2]
    sectors, inners = lax.axis_size("sector"), lax.axis_size("inner")
    chunks = 2 if sectors * inners <= 16 else 1
    copies = chunks * (2 * (sectors + 1) * (inners + 1) + 2 * sectors * inners)
    out = jax.ShapeDtypeStruct((1, rows, cols), jnp.bfloat16)
    vmem = pl.BlockSpec(memory_space=pltpu.VMEM)
    smem = pl.BlockSpec(memory_space=pltpu.SMEM)
    hbm = pl.BlockSpec(memory_space=pl.ANY)
    return pl.pallas_call(
        functools.partial(kernel, sectors, inners, chunks),
        out_shape=(out, out),
        in_specs=[vmem, hbm, hbm, smem, smem],
        out_specs=(vmem, vmem),
        scratch_shapes=[
            pltpu.VMEM((width // cols, sectors, width, cols), jnp.bfloat16),
            pltpu.VMEM((width // cols, sectors, width, cols), jnp.bfloat16),
            pltpu.VMEM(left_env.shape[1:], jnp.bfloat16),
            pltpu.VMEM(right_env.shape[1:], jnp.bfloat16),
            pltpu.VMEM((rows, cols), jnp.float32),
            pltpu.SemaphoreType.DMA((2,)),
            pltpu.SemaphoreType.DMA((2, copies)),
            pltpu.SemaphoreType.DMA((2, chunks, width // cols, sectors, inners)),
        ],
        compiler_params=pltpu.CompilerParams(
            collective_id=0, has_side_effects=True, vmem_limit_bytes=56 * 1024 * 1024
        ),
    )(wave_blocks, left_env, right_env, source_pairs, block_sizes)


def solution(mesh):
    return jax.shard_map(
        body,
        mesh=mesh,
        in_specs=(
            P(("copies", "sector"), "inner", None),
            P(("copies", "sector"), None, "inner", None),
            P(("copies", "sector"), None, "pair", None),
            P(("copies", "sector"), None),
            P("copies"),
        ),
        out_specs=(
            P(("copies", "sector"), "inner", "pair"),
            P(("copies", "sector"), "inner", "pair"),
        ),
        check_vma=False,
    )
```

```python
import functools

import jax
import jax.numpy as jnp
from jax import lax
from jax.experimental import pallas as pl
from jax.experimental.pallas import tpu as pltpu
from jax.sharding import PartitionSpec as P

MESH = pl.DeviceIdType.MESH


def kernel(
    sectors, inners, chunks, wave_ref, left_hbm, right_hbm, src_ref, size_ref, first_ref, second_ref,
    field, sigma, left_ref, right_ref, total, load_sem, send_sem, recv_sem,
):
    _, rows, width = wave_ref.shape
    terms, cols = right_ref.shape[0], right_ref.shape[1]
    s = lax.axis_index("sector")
    i = lax.axis_index("inner")
    p = lax.axis_index("pair")
    other = 1 - p
    after = [lax.rem(i + step, inners) for step in range(1, inners)]
    before = [lax.rem(i + inners - step, inners) for step in range(1, inners)]

    loads = (
        pltpu.make_async_copy(left_hbm.at[0], left_ref, load_sem.at[0]),
        pltpu.make_async_copy(right_hbm.at[0], right_ref, load_sem.at[1]),
    )
    for load in loads:
        load.start()

    barrier = pltpu.get_barrier_semaphore()
    up, down = s + 1, s - 1
    has_up, has_down = up < sectors, down >= 0
    for near, there in ((has_up, up), (has_down, down)):
        @pl.when(near)
        def _(there=there):
            pl.semaphore_signal(barrier, inc=1, device_id={"sector": there}, device_id_type=MESH)
    for there in after:
        pl.semaphore_signal(barrier, inc=1, device_id={"inner": there}, device_id_type=MESH)
    pl.semaphore_signal(barrier, inc=1, device_id={"pair": other}, device_id_type=MESH)

    depth = rows // chunks

    def part(buffer, half, sector, inner, chunk):
        start = pl.multiple_of(inner * rows + chunk * depth, depth)
        return buffer.at[half, sector, pl.ds(start, depth), :]

    size = size_ref[s]
    own_row = pl.multiple_of(i * rows, rows)
    row_ids = own_row + lax.broadcasted_iota(jnp.int32, (rows, cols), 0)
    col_ids = lax.broadcasted_iota(jnp.int32, (rows, cols), 1)
    row_live = row_ids < size
    for half in range(width // cols):
        live = row_live & (col_ids + half * cols < size)
        piece = wave_ref[0, :, half * cols:(half + 1) * cols].astype(jnp.float32)
        field[half, s, pl.ds(own_row, rows), :] = jnp.where(live, piece, 0.0).astype(jnp.bfloat16)

    ends = lax.div(s + sectors - 1, sectors) + lax.div(2 * sectors - 2 - s, sectors)
    pl.semaphore_wait(barrier, inners + ends)

    def guarded(cond, work):
        if cond is None:
            work()
        else:
            pl.when(cond)(work)

    def gather(buffer, phase, share_own):
        started = []

        def send(cond, half, sector, inner, chunk, to):
            number = len(started)

            def make():
                ref = part(buffer, half, sector, inner, chunk)
                return pltpu.make_async_remote_copy(
                    src_ref=ref, dst_ref=ref, send_sem=send_sem.at[phase, number],
                    recv_sem=recv_sem.at[phase, chunk, half, sector, inner],
                    device_id=to, device_id_type=MESH,
                )

            started.append((cond, make))
            make().start()

        def arrive(half, sector, inner, chunk):
            ref = part(buffer, half, sector, inner, chunk)
            pltpu.make_async_remote_copy(
                src_ref=ref, dst_ref=ref, send_sem=send_sem.at[phase, 0],
                recv_sem=recv_sem.at[phase, chunk, half, sector, inner],
                device_id={"pair": other}, device_id_type=MESH,
            ).wait_recv()

        def spread(cond, sector, chunk):
            for there in after:
                send(cond, p, sector, i, chunk, {"inner": there})

        def from_inner(cond, sector, chunk):
            def work():
                for there in before:
                    arrive(p, sector, there, chunk)
                    send(cond, p, sector, there, chunk, {"pair": other})
            guarded(cond, work)

        def from_sector(cond, sector, further, onward, chunk):
            both = cond & onward

            def work():
                arrive(p, sector, i, chunk)
                pl.when(onward)(lambda: send(both, p, sector, i, chunk, {"sector": further}))
                spread(cond, sector, chunk)
                send(cond, p, sector, i, chunk, {"pair": other})
            guarded(cond, work)

        for chunk in range(chunks):
            pl.when(has_up)(lambda: send(has_up, p, s, i, chunk, {"sector": up}))
            pl.when(has_down)(lambda: send(has_down, p, s, i, chunk, {"sector": down}))
            spread(None, s, chunk)
            if share_own:
                send(None, p, s, i, chunk, {"pair": other})

        late = [(None, s)]
        for step in range(1, sectors):
            below, above = s - step >= 0, s + step < sectors
            arriving = [(below, s - step), (above, s + step)]
            for chunk in range(chunks):
                from_sector(*arriving[0], up, has_up, chunk)
                from_sector(*arriving[1], down, has_down, chunk)
            late += arriving
        for cond, sector in late:
            for chunk in range(chunks):
                from_inner(cond, sector, chunk)

        for sector in range(sectors):
            for inner in range(inners):
                for chunk in range(chunks):
                    wait = functools.partial(arrive, other, sector, inner, chunk)
                    guarded(None if share_own else (sector != s) | (inner != i), wait)
        for cond, make in started:
            guarded(cond, lambda make=make: make().wait_send())

    def dot(a, b, dims):
        return lax.dot_general(a, b, (dims, ((), ())), preferred_element_type=jnp.float32)

    def apply():
        total[...] = jnp.zeros_like(total)

        def term(k, carry):
            source = src_ref[0, k]
            half = sum(
                dot(field[q, source], right_ref[k, :, q * cols:(q + 1) * cols], ((1,), (1,)))
                for q in range(width // cols)
            ).astype(jnp.bfloat16)
            total[...] += dot(left_ref[k], half, ((1,), (0,)))
            return carry

        lax.fori_loop(0, terms, term, 0, unroll=terms)
        live = row_live & (col_ids + p * cols < size)
        return jnp.where(live, total[...], 0.0).astype(jnp.bfloat16)

    gather(field, 0, False)
    for load in loads:
        load.wait()
    first = apply()
    first_ref[0] = first
    sigma[p, s, pl.ds(own_row, rows), :] = first
    gather(sigma, 1, True)

    blocks = [(q, t) for q in range(width // cols) for t in range(sectors)]

    def fold(x):
        return jnp.sum(x.reshape(-1, 8, cols), axis=0)

    def sums(n, carry):
        q, t = n // sectors, lax.rem(n, sectors)
        w = field[q, t].astype(jnp.float32)
        g = sigma[q, t].astype(jnp.float32)
        return (carry[0] + fold(w * w), carry[1] + fold(w * g), carry[2] + fold(g * g))

    zero = jnp.zeros((8, cols), jnp.float32)
    self_norm, correlation, sigma_norm = (
        jnp.sum(x) for x in lax.fori_loop(0, len(blocks), sums, (zero, zero, zero))
    )
    self_norm, correlation, sigma_norm = (
        jnp.full((8, cols), x, jnp.float32) for x in (self_norm, correlation, sigma_norm)
    )
    rayleigh = correlation / self_norm
    residual_sq = sigma_norm - 2.0 * rayleigh * correlation + rayleigh * rayleigh * self_norm
    scale = lax.rsqrt(residual_sq / (sectors * width * width) + 1e-06)
    rayleigh, scale = rayleigh[:1], scale[:1]

    def correct(n, carry):
        q, t = n // sectors, lax.rem(n, sectors)
        w = field[q, t].astype(jnp.float32)
        g = sigma[q, t].astype(jnp.float32)
        field[q, t] = ((g - rayleigh * w) * scale).astype(jnp.bfloat16)
        return carry

    lax.fori_loop(0, len(blocks), correct, 0)
    second_ref[0] = apply()


def body(wave_blocks, left_env, right_env, source_pairs, block_sizes):
    _, rows, width = wave_blocks.shape
    terms, cols = right_env.shape[1], right_env.shape[2]
    sectors, inners = lax.axis_size("sector"), lax.axis_size("inner")
    chunks = 2 if sectors * inners <= 16 else 1
    copies = chunks * (2 * (sectors + 1) * (inners + 1) + 2 * sectors * inners)
    out = jax.ShapeDtypeStruct((1, rows, cols), jnp.bfloat16)
    vmem = pl.BlockSpec(memory_space=pltpu.VMEM)
    smem = pl.BlockSpec(memory_space=pltpu.SMEM)
    hbm = pl.BlockSpec(memory_space=pl.ANY)
    outs = pl.pallas_call(
        functools.partial(kernel, sectors, inners, chunks),
        out_shape=(out, out),
        in_specs=[vmem, hbm, hbm, smem, smem],
        out_specs=(vmem, vmem),
        scratch_shapes=[
            pltpu.VMEM((width // cols, sectors, width, cols), jnp.bfloat16),
            pltpu.VMEM((width // cols, sectors, width, cols), jnp.bfloat16),
            pltpu.VMEM(left_env.shape[1:], jnp.bfloat16),
            pltpu.VMEM(right_env.shape[1:], jnp.bfloat16),
            pltpu.VMEM((rows, cols), jnp.float32),
            pltpu.SemaphoreType.DMA((2,)),
            pltpu.SemaphoreType.DMA((2, copies)),
            pltpu.SemaphoreType.DMA((2, chunks, width // cols, sectors, inners)),
        ],
        compiler_params=pltpu.CompilerParams(
            collective_id=0, has_side_effects=True, vmem_limit_bytes=56 * 1024 * 1024
        ),
    )(wave_blocks, left_env, right_env, source_pairs, block_sizes)

    def hand_on(a, b, c, d, sem):
        moves = [pltpu.make_async_copy(a, c, sem.at[0]), pltpu.make_async_copy(b, d, sem.at[1])]
        for move in moves:
            move.start()
        for move in moves:
            move.wait()

    return pl.pallas_call(
        hand_on,
        out_shape=(out, out),
        in_specs=[vmem, vmem],
        out_specs=(hbm, hbm),
        scratch_shapes=[pltpu.SemaphoreType.DMA((2,))],
    )(*outs)


def solution(mesh):
    return jax.shard_map(
        body,
        mesh=mesh,
        in_specs=(
            P(("copies", "sector"), "inner", None),
            P(("copies", "sector"), None, "inner", None),
            P(("copies", "sector"), None, "pair", None),
            P(("copies", "sector"), None),
            P("copies"),
        ),
        out_specs=(
            P(("copies", "sector"), "inner", "pair"),
            P(("copies", "sector"), "inner", "pair"),
        ),
        check_vma=False,
    )
```

```python
import functools

import jax
import jax.numpy as jnp
from jax import lax
from jax.experimental import pallas as pl
from jax.experimental.pallas import tpu as pltpu
from jax.sharding import PartitionSpec as P

MESH = pl.DeviceIdType.MESH


def kernel(
    sectors, inners, chunks, wave_ref, left_hbm, right_hbm, src_ref, size_ref, first_ref, second_ref,
    field, sigma, left_ref, right_ref, halfway, load_sem, send_sem, recv_sem,
):
    _, rows, width = wave_ref.shape
    terms, cols = right_ref.shape[0], right_ref.shape[1]
    s = lax.axis_index("sector")
    i = lax.axis_index("inner")
    p = lax.axis_index("pair")
    other = 1 - p
    after = [lax.rem(i + step, inners) for step in range(1, inners)]
    before = [lax.rem(i + inners - step, inners) for step in range(1, inners)]

    loads = (
        pltpu.make_async_copy(left_hbm.at[0], left_ref, load_sem.at[0]),
        pltpu.make_async_copy(right_hbm.at[0], right_ref, load_sem.at[1]),
    )
    for load in loads:
        load.start()

    barrier = pltpu.get_barrier_semaphore()
    up, down = s + 1, s - 1
    has_up, has_down = up < sectors, down >= 0
    for near, there in ((has_up, up), (has_down, down)):
        @pl.when(near)
        def _(there=there):
            pl.semaphore_signal(barrier, inc=1, device_id={"sector": there}, device_id_type=MESH)
    for there in after:
        pl.semaphore_signal(barrier, inc=1, device_id={"inner": there}, device_id_type=MESH)
    pl.semaphore_signal(barrier, inc=1, device_id={"pair": other}, device_id_type=MESH)

    depth = rows // chunks

    def part(buffer, half, sector, inner, chunk):
        start = pl.multiple_of(inner * rows + chunk * depth, depth)
        return buffer.at[half, sector, pl.ds(start, depth), :]

    size = size_ref[s]
    own_row = pl.multiple_of(i * rows, rows)
    row_ids = own_row + lax.broadcasted_iota(jnp.int32, (rows, cols), 0)
    col_ids = lax.broadcasted_iota(jnp.int32, (rows, cols), 1)
    row_live = row_ids < size
    for half in range(width // cols):
        live = row_live & (col_ids + half * cols < size)
        piece = wave_ref[0, :, half * cols:(half + 1) * cols].astype(jnp.float32)
        field[half, s, pl.ds(own_row, rows), :] = jnp.where(live, piece, 0.0).astype(jnp.bfloat16)

    ends = lax.div(s + sectors - 1, sectors) + lax.div(2 * sectors - 2 - s, sectors)
    pl.semaphore_wait(barrier, inners + ends)

    def guarded(cond, work):
        if cond is None:
            work()
        else:
            pl.when(cond)(work)

    def gather(buffer, phase, share_own, prepare=None):
        started = []

        def send(cond, half, sector, inner, chunk, to):
            number = len(started)

            def make():
                ref = part(buffer, half, sector, inner, chunk)
                return pltpu.make_async_remote_copy(
                    src_ref=ref, dst_ref=ref, send_sem=send_sem.at[phase, number],
                    recv_sem=recv_sem.at[phase, chunk, half, sector, inner],
                    device_id=to, device_id_type=MESH,
                )

            started.append((cond, make))
            make().start()

        def arrive(half, sector, inner, chunk):
            ref = part(buffer, half, sector, inner, chunk)
            pltpu.make_async_remote_copy(
                src_ref=ref, dst_ref=ref, send_sem=send_sem.at[phase, 0],
                recv_sem=recv_sem.at[phase, chunk, half, sector, inner],
                device_id={"pair": other}, device_id_type=MESH,
            ).wait_recv()

        def spread(cond, sector, chunk):
            for there in after:
                send(cond, p, sector, i, chunk, {"inner": there})

        def from_inner(cond, sector, chunk):
            def work():
                for there in before:
                    arrive(p, sector, there, chunk)
                    send(cond, p, sector, there, chunk, {"pair": other})
            guarded(cond, work)

        def from_sector(cond, sector, further, onward, chunk):
            both = cond & onward

            def work():
                arrive(p, sector, i, chunk)
                pl.when(onward)(lambda: send(both, p, sector, i, chunk, {"sector": further}))
                spread(cond, sector, chunk)
                send(cond, p, sector, i, chunk, {"pair": other})
            guarded(cond, work)

        for chunk in range(chunks):
            if prepare is not None:
                prepare(chunk)
            pl.when(has_up)(lambda: send(has_up, p, s, i, chunk, {"sector": up}))
            pl.when(has_down)(lambda: send(has_down, p, s, i, chunk, {"sector": down}))
            spread(None, s, chunk)
            if share_own:
                send(None, p, s, i, chunk, {"pair": other})

        late = [(None, s)]
        for step in range(1, sectors):
            below, above = s - step >= 0, s + step < sectors
            arriving = [(below, s - step), (above, s + step)]
            for chunk in range(chunks):
                from_sector(*arriving[0], up, has_up, chunk)
                from_sector(*arriving[1], down, has_down, chunk)
            late += arriving
        for cond, sector in late:
            for chunk in range(chunks):
                from_inner(cond, sector, chunk)

        for sector in range(sectors):
            for inner in range(inners):
                for chunk in range(chunks):
                    wait = functools.partial(arrive, other, sector, inner, chunk)
                    guarded(None if share_own else (sector != s) | (inner != i), wait)
        def finish():
            for cond, make in started:
                guarded(cond, lambda make=make: make().wait_send())

        return finish

    def dot(a, b, dims):
        return lax.dot_general(a, b, (dims, ((), ())), preferred_element_type=jnp.float32)

    def contract():
        def term(k, carry):
            source = src_ref[0, k]
            halfway[k] = sum(
                dot(field[q, source], right_ref[k, :, q * cols:(q + 1) * cols], ((1,), (1,)))
                for q in range(width // cols)
            ).astype(jnp.bfloat16)
            return carry

        lax.fori_loop(0, terms, term, 0, unroll=terms)

    def finished(chunk):
        here = slice(chunk * depth, (chunk + 1) * depth)
        total = sum(dot(left_ref[k, here, :], halfway[k], ((1,), (0,))) for k in range(terms))
        live = row_live[here] & (col_ids[here] + p * cols < size)
        return jnp.where(live, total, 0.0).astype(jnp.bfloat16)

    def first_rows(chunk):
        first = finished(chunk)
        first_ref[0, chunk * depth:(chunk + 1) * depth, :] = first
        sigma[p, s, pl.ds(pl.multiple_of(own_row + chunk * depth, depth), depth), :] = first

    field_sent = gather(field, 0, False)
    for load in loads:
        load.wait()
    contract()
    sigma_sent = gather(sigma, 1, True, first_rows)

    blocks = [(q, t) for q in range(width // cols) for t in range(sectors)]

    def fold(x):
        return jnp.sum(x.reshape(-1, 8, cols), axis=0)

    def sums(n, carry):
        q, t = n // sectors, lax.rem(n, sectors)
        w = field[q, t].astype(jnp.float32)
        g = sigma[q, t].astype(jnp.float32)
        return (carry[0] + fold(w * w), carry[1] + fold(w * g), carry[2] + fold(g * g))

    zero = jnp.zeros((8, cols), jnp.float32)
    self_norm, correlation, sigma_norm = (
        jnp.sum(x) for x in lax.fori_loop(0, len(blocks), sums, (zero, zero, zero))
    )
    self_norm, correlation, sigma_norm = (
        jnp.full((8, cols), x, jnp.float32) for x in (self_norm, correlation, sigma_norm)
    )
    rayleigh = correlation / self_norm
    residual_sq = sigma_norm - 2.0 * rayleigh * correlation + rayleigh * rayleigh * self_norm
    scale = lax.rsqrt(residual_sq / (sectors * width * width) + 1e-06)
    rayleigh, scale = rayleigh[:1], scale[:1]

    def correct(n, carry):
        q, t = n // sectors, lax.rem(n, sectors)
        w = field[q, t].astype(jnp.float32)
        g = sigma[q, t].astype(jnp.float32)
        field[q, t] = ((g - rayleigh * w) * scale).astype(jnp.bfloat16)
        return carry

    field_sent()
    lax.fori_loop(0, len(blocks), correct, 0)
    contract()
    for chunk in range(chunks):
        second_ref[0, chunk * depth:(chunk + 1) * depth, :] = finished(chunk)
    sigma_sent()


def body(wave_blocks, left_env, right_env, source_pairs, block_sizes):
    _, rows, width = wave_blocks.shape
    terms, cols = right_env.shape[1], right_env.shape[2]
    sectors, inners = lax.axis_size("sector"), lax.axis_size("inner")
    chunks = 2 if sectors * inners <= 16 else 1
    copies = chunks * (2 * (sectors + 1) * (inners + 1) + 2 * sectors * inners)
    out = jax.ShapeDtypeStruct((1, rows, cols), jnp.bfloat16)
    vmem = pl.BlockSpec(memory_space=pltpu.VMEM)
    smem = pl.BlockSpec(memory_space=pltpu.SMEM)
    hbm = pl.BlockSpec(memory_space=pl.ANY)
    outs = pl.pallas_call(
        functools.partial(kernel, sectors, inners, chunks),
        out_shape=(out, out),
        in_specs=[vmem, hbm, hbm, smem, smem],
        out_specs=(vmem, vmem),
        scratch_shapes=[
            pltpu.VMEM((width // cols, sectors, width, cols), jnp.bfloat16),
            pltpu.VMEM((width // cols, sectors, width, cols), jnp.bfloat16),
            pltpu.VMEM(left_env.shape[1:], jnp.bfloat16),
            pltpu.VMEM(right_env.shape[1:], jnp.bfloat16),
            pltpu.VMEM((terms, width, cols), jnp.bfloat16),
            pltpu.SemaphoreType.DMA((2,)),
            pltpu.SemaphoreType.DMA((2, copies)),
            pltpu.SemaphoreType.DMA((2, chunks, width // cols, sectors, inners)),
        ],
        compiler_params=pltpu.CompilerParams(
            collective_id=0, has_side_effects=True, vmem_limit_bytes=56 * 1024 * 1024
        ),
    )(wave_blocks, left_env, right_env, source_pairs, block_sizes)

    def hand_on(a, b, c, d, sem):
        moves = [pltpu.make_async_copy(a, c, sem.at[0]), pltpu.make_async_copy(b, d, sem.at[1])]
        for move in moves:
            move.start()
        for move in moves:
            move.wait()

    return pl.pallas_call(
        hand_on,
        out_shape=(out, out),
        in_specs=[vmem, vmem],
        out_specs=(hbm, hbm),
        scratch_shapes=[pltpu.SemaphoreType.DMA((2,))],
    )(*outs)


def solution(mesh):
    return jax.shard_map(
        body,
        mesh=mesh,
        in_specs=(
            P(("copies", "sector"), "inner", None),
            P(("copies", "sector"), None, "inner", None),
            P(("copies", "sector"), None, "pair", None),
            P(("copies", "sector"), None),
            P("copies"),
        ),
        out_specs=(
            P(("copies", "sector"), "inner", "pair"),
            P(("copies", "sector"), "inner", "pair"),
        ),
        check_vma=False,
    )
```
